128 devices in a mesh: lon: 8 (over z_lo, x), lat: 16 (over z_hi, y, core).
Axes of the slice: x: 4, y: 4, z: 4 (z_hi: 2, z_lo: 2; z = z_hi * 2 + z_lo), core: 2. Of those that a mesh axis runs over, the one named last changes fastest.
Arguments:
- tokens: float32 [2, 240, 800, 512], P(None, 'lat', 'lon'), may hold values from -6 to 6
- ln_gain: float32 [512], replicated, may hold values from 0.1 to 1.9
- ln_shift: float32 [512], replicated, may hold values from -3 to 3
- w_qkv: float32 [512, 1536], replicated, may hold values from -0.25 to 0.25
- w_out: float32 [512, 512], replicated, may hold values from -0.25 to 0.25
- region_ids: int32 [240], replicated, may hold values from 0 to 29, never falling along the last dimension, each value on 1 to 16 neighbouring positions
- position_bias: float32 [48, 16, 100, 100], P('lat'), may hold values from -4 to 400
Outputs:
- updated: float32 [2, 240, 800, 512], P(None, 'lat', 'lon')
The draws below stay inside these ranges and needn't reach their ends.
Inputs may be any that keep to these rules, and one draw needn't show every extreme that they name: `region_ids`: ids never fall along latitude; each id covers 1 to 16 consecutive rows, one exactly 16.
All inputs are finite; a program needn't handle non-finite values.
Results may differ from the reference program's by a relative error of at most 0.0003.
Values sent between devices are 32-bit elements; how exact they have to be, the bound alone decides.
No kernel may reach another device: no remote copies, remote signals or barrier semaphores. Data moves between devices by JAX's collectives and lax.ppermute only.
A program may use at most 192 MiB of HBM per device.

```python
import math
import jax
import jax.numpy as jnp
import numpy as np
from jax import lax

D = 512
HEADS = 16
LEV = 2
WLON = 10
WLAT = 5
WTOK = 100
NLON = 800
NLAT = 240
NWLAT = 48


def draw_position_bias(key, part):
    key = jax.random.fold_in(key, 11)
    key_base = jax.random.fold_in(key, 0)
    table = jnp.clip(jax.random.normal(key_base, (NWLAT, HEADS, WTOK, WTOK), jnp.float32), -4.0, 4.0)
    return table.astype(jnp.float32)


def block_levels(own_key, dims, cuts, low, high):
    def one(axis_at, blocks):
        draws = jax.random.uniform(jax.random.fold_in(jax.random.fold_in(own_key, 6), axis_at), (blocks,), jnp.float32, low / len(cuts), high / len(cuts))
        return jnp.repeat(jnp.exp(draws), dims[axis_at] // blocks).reshape((-1,) + (1,) * (len(dims) - axis_at - 1))

    level = one(*cuts[0])
    for cut in cuts[1:]:
        level = level * one(*cut)
    return level


def profile(amount, total, bound, lean):
    portions = [(1 << 20) // math.isqrt(standing ** lean) + 1 for standing in range(2, amount + 1)]
    rest, given = total - bound - (amount - 1), [1] * (amount - 1)
    while rest > 0:
        movable = [i for i in range(amount - 1) if given[i] < bound]
        mass, left = sum([portions[i] for i in movable]), rest
        for i in movable:
            addition = min(bound - given[i], max(1, left * portions[i] // mass), rest)
            given[i] = given[i] + addition
            rest = rest - addition
    return np.array([bound] + given)


def uneven_parts(rng, amount, total, limit, slope):
    if amount == 2:
        one = jax.random.randint(rng, (), max(1, total - limit), min(limit, total - 1) + 1)
        return jnp.stack([one, total - one])
    tallies = jnp.asarray(profile(amount, total, limit, slope), jnp.int32)
    pairs = (amount - 1) // 2
    giver, sink = tallies[1:1 + 2 * pairs:2], tallies[2:2 + 2 * pairs:2]
    slack = jnp.minimum(giver - 1, limit - sink)
    moved = jax.random.randint(jax.random.fold_in(rng, 1), (pairs,), 0, 1 << 20) % (slack + 1)
    tallies = tallies.at[1:1 + 2 * pairs:2].set(giver - moved).at[2:2 + 2 * pairs:2].set(sink + moved)
    return tallies[jax.random.permutation(jax.random.fold_in(rng, 2), amount)]


def normal_values(stream_key, dims, scale, bound, pieces=(), kind=jnp.bfloat16):
    level = block_levels(stream_key, dims, pieces, -0.22, 0.18) if pieces else 1.0
    drawn = jax.random.normal(stream_key, dims, jnp.float32) * scale * level
    return jnp.minimum(jnp.maximum(drawn, -bound), bound).astype(kind)


def setup_inputs(seed: int = 0) -> dict:
    arg_keys = jax.random.split(jax.random.key(seed), 8)
    tokens = normal_values(arg_keys[0], (LEV, NLAT, NLON, D), 1.0, 6.0, ((1, 16), (2, 8)), jnp.float32)
    ln_gain = jnp.clip(1.0 + 0.18 * jax.random.normal(arg_keys[1], (D,), jnp.float32), 0.1, 1.9)
    ln_shift = normal_values(arg_keys[2], (D,), 0.5, 3.0, (), jnp.float32)
    w_qkv = normal_values(arg_keys[3], (D, 3 * D), D ** -0.5, 0.25, (), jnp.float32)
    w_out = normal_values(arg_keys[4], (D, D), D ** -0.5, 0.25, (), jnp.float32)
    region_ids = jnp.searchsorted(jnp.cumsum(uneven_parts(arg_keys[5], NLAT // 8, NLAT, 16, 1)), jnp.arange(NLAT), side="right").astype(jnp.int32)
    position_bias = draw_position_bias(jax.random.fold_in(arg_keys[7], 71), 0)
    return {"tokens": tokens, "ln_gain": ln_gain, "ln_shift": ln_shift, "w_qkv": w_qkv, "w_out": w_out, "region_ids": region_ids, "position_bias": position_bias}


def layer_norm(inputs, gain_vec, shift_vec):
    center = lax.optimization_barrier(jnp.mean(inputs, axis=-1, keepdims=True))
    deviate = inputs - center
    spread = lax.optimization_barrier(jnp.mean(deviate * deviate, axis=-1, keepdims=True))
    return deviate * lax.rsqrt(spread + 1e-05) * gain_vec + shift_vec

def to_windows(field_data):
    levels, row_count, col_count, feat_count = field_data.shape
    field_data = field_data.reshape(levels, row_count // WLAT, WLAT, col_count // WLON, WLON, feat_count)
    field_data = field_data.transpose(1, 3, 0, 2, 4, 5)
    return field_data.reshape(row_count // WLAT, col_count // WLON, levels * WLAT * WLON, feat_count)

def from_windows(field_data, levels):
    band_count, across, tok_count, feat_count = field_data.shape
    field_data = field_data.reshape(band_count, across, levels, WLAT, WLON, feat_count)
    field_data = field_data.transpose(2, 0, 3, 1, 4, 5)
    return field_data.reshape(levels, band_count * WLAT, across * WLON, feat_count)

def window_ids(row_ids, levels):
    band_count = row_ids.shape[0] // WLAT
    id_grid = jnp.broadcast_to(row_ids.reshape(band_count, 1, WLAT, 1), (band_count, levels, WLAT, WLON))
    return id_grid.reshape(band_count, levels * WLAT * WLON)

def attend(packed, token_ids, band_bias):
    band_count, across, tok_count, _ = packed.shape
    head_dim = D // HEADS
    queries = packed[..., :D].reshape(band_count, across, tok_count, HEADS, head_dim)
    key_rows = packed[..., D:2 * D].reshape(band_count, across, tok_count, HEADS, head_dim)
    values = packed[..., 2 * D:].reshape(band_count, across, tok_count, HEADS, head_dim)
    scores = jnp.einsum('abqhc,abkhc->abhqk', queries, key_rows, precision=lax.Precision.HIGHEST)
    scores = scores * head_dim ** (-0.5) + band_bias[:, None]
    allowed = token_ids[:, None, None, :, None] == token_ids[:, None, None, None, :]
    scores = jnp.where(allowed, scores, -1e+30)
    scores = scores - lax.optimization_barrier(jnp.max(scores, axis=-1, keepdims=True))
    weights = jnp.exp(scores)
    weights = weights / lax.optimization_barrier(jnp.sum(weights, axis=-1, keepdims=True))
    mixed_heads = jnp.einsum('abhqk,abkhc->abqhc', weights, values, precision=lax.Precision.HIGHEST)
    return mixed_heads.reshape(band_count, across, tok_count, D)

def reference(tokens, ln_gain, ln_shift, w_qkv, w_out, region_ids, position_bias):
    levels = tokens.shape[0]
    half_lat = WLAT // 2
    half_lon = WLON // 2
    rolled = jnp.roll(tokens, (-half_lat, -half_lon), axis=(1, 2))
    rolled_ids = jnp.roll(region_ids, -half_lat)

    def one_band(band_index):
        row_start = band_index * WLAT
        band_rows = lax.dynamic_slice_in_dim(rolled, row_start, WLAT, 1)
        band_ids = lax.dynamic_slice_in_dim(rolled_ids, row_start, WLAT, 0)
        band_bias = lax.dynamic_slice_in_dim(position_bias, band_index, 1, 0)
        normed = layer_norm(band_rows, ln_gain, ln_shift)
        packed = jnp.dot(normed, w_qkv, precision=lax.Precision.HIGHEST, preferred_element_type=jnp.float32)
        mixed_heads = attend(to_windows(packed), window_ids(band_ids, levels), band_bias)
        projected = jnp.dot(mixed_heads, w_out, precision=lax.Precision.HIGHEST, preferred_element_type=jnp.float32)
        return from_windows(projected, levels)
    stacked = lax.map(one_band, jnp.arange(NWLAT, dtype=jnp.int32))
    shifted = stacked.transpose(1, 0, 2, 3, 4).reshape(levels, NLAT, NLON, D)
    return tokens + jnp.roll(shifted, (half_lat, half_lon), axis=(1, 2))
```

```python
import functools
import math

import jax
import jax.numpy as jnp
from jax import lax
from jax.experimental import pallas as pl
from jax.experimental.pallas import tpu as pltpu
from jax.sharding import PartitionSpec as P

D = 512
HEADS = 16
WLON = 10
WLAT = 5
HALF_LAT = WLAT // 2
HALF_LON = WLON // 2
ROWS = 15
COLS = 100
BANDS = ROWS // WLAT
ACROSS = COLS // WLON
SUB = 8
CELLS = WLAT * WLON
CELL_PAD = 56
TOK_PAD = 2 * CELL_PAD
SLAB = CELL_PAD * SUB
S_COLS = COLS - HALF_LON
NEG = -1e30
LOG2E = math.log2(math.e)
QSCALE = LOG2E / math.sqrt(D // HEADS)
BF = jnp.bfloat16
F32 = jnp.float32


def hi_lo(x):
    hi = x.astype(BF)
    lo = (x - hi.astype(F32)).astype(BF)
    return hi, lo


def pieces(band, win):
    out = []
    for i in range(WLAT):
        row = WLAT * band + HALF_LAT + i
        col = WLON * win + HALF_LON
        wide = min(WLON, COLS - col)
        south = row >= ROWS
        if south:
            out.append((i * WLON, "s", (row - ROWS) * S_COLS + col - HALF_LON, wide))
        else:
            out.append((i * WLON, "t", row * COLS + col, wide))
        if wide < WLON:
            if south:
                out.append((i * WLON + wide, "c", (row - ROWS) * HALF_LON, WLON - wide))
            else:
                out.append((i * WLON + wide, "e", (row - HALF_LAT) * HALF_LON, WLON - wide))
    return out


def dot(a, b):
    return lax.dot_general(a, b, (((1,), (0,)), ((), ())), preferred_element_type=F32)


def dot_t(a, b):
    return lax.dot_general(a, b, (((1,), (1,)), ((), ())), preferred_element_type=F32)


def group_kernel(runs, halo, aliased, *refs):
    refs = list(refs)
    ids_ref, tok_hbm = refs[:2]
    del refs[:2]
    srcs = {"t": tok_hbm}
    if halo:
        srcs.update(zip("sec", refs[:3]))
        del refs[:3]
    gain_ref, shift_ref, wqkv_hbm, wout_hbm, bias_hbm = refs[:5]
    del refs[:5]
    if aliased:
        del refs[0]
    dsts = {"t": refs.pop(0)}
    if halo:
        dsts.update(zip("sec", refs[:3]))
        del refs[:3]
    (tok, stage_q, stage_o, bias_v, wq, wo, xcat, qkv, hcat, biasm,
     sem_tok, sem_w, sem_b, sem_out) = refs

    wins = [(b, w) for b, ws in runs for w in ws]
    nw = len(wins)
    rows_all = nw * TOK_PAD

    def move(i, srcs_or_dsts, into, sem):
        band, win = wins[i]
        for cell, name, start, count in pieces(band, win):
            here = tok.at[pl.ds(i * SLAB + cell * SUB, count * SUB)]
            there = srcs_or_dsts[name].at[pl.ds(start * SUB, count * SUB)]
            if into:
                pltpu.make_async_copy(there, here, sem).start()
            else:
                pltpu.make_async_copy(here, there, sem).start()

    for i in range(nw):
        move(i, srcs, True, sem_tok.at[i])
    copy_q = pltpu.make_async_copy(wqkv_hbm, stage_q, sem_w.at[0])
    copy_o = pltpu.make_async_copy(wout_hbm, stage_o, sem_w.at[1])
    copy_q.start()
    copies_b = []
    for j, (b, _) in enumerate(runs):
        c = pltpu.make_async_copy(
            bias_hbm.at[pl.ds(b * 1600, 1600)], bias_v.at[j, pl.ds(0, 1600)], sem_b.at[j])
        c.start()
        copies_b.append(c)
    copy_o.start()

    gain = gain_ref[...].reshape(1, D)
    shift = shift_ref[...].reshape(1, D)
    pad_rows = jnp.zeros(((CELL_PAD - CELLS) * SUB, 128), F32)

    def norm_window(i, _):
        base = pl.multiple_of(i * SLAB, SLAB)
        pltpu.make_async_copy(
            tok_hbm.at[pl.ds(0, CELLS * SUB)], tok.at[pl.ds(base, CELLS * SUB)], sem_tok.at[i]).wait()
        tok[pl.ds(base + CELLS * SUB, (CELL_PAD - CELLS) * SUB), :] = pad_rows
        parts = [
            jnp.concatenate(
                [tok[pl.ds(base + g * 2 + lev, CELL_PAD, stride=SUB), :] for lev in range(2)], axis=0)
            for g in range(4)
        ]
        center = jnp.sum(parts[0] + parts[1] + parts[2] + parts[3], axis=1, keepdims=True) * (1.0 / D)
        parts = [p - center for p in parts]
        sq = [p * p for p in parts]
        spread = jnp.sum(sq[0] + sq[1] + sq[2] + sq[3], axis=1, keepdims=True) * (1.0 / D)
        scale = lax.rsqrt(spread + 1e-05)
        r = pl.ds(pl.multiple_of(i * TOK_PAD, TOK_PAD), TOK_PAD)
        for g in range(4):
            cols = slice(g * 128, (g + 1) * 128)
            y = parts[g] * scale * gain[:, cols] + shift[:, cols]
            hi, lo = hi_lo(y)
            xcat[r, g * 128:(g + 1) * 128] = hi
            xcat[r, D + g * 128:D + (g + 1) * 128] = lo
        return 0

    lax.fori_loop(0, nw, norm_window, 0)

    copy_q.wait()

    def split_q(i, _):
        r = pl.ds(pl.multiple_of(i * 16, 16), 16)
        for part in range(3):
            x = stage_q[r, part * D:(part + 1) * D]
            if part == 0:
                x = x * QSCALE
            hi, lo = hi_lo(x)
            wq[r, part * D:(part + 1) * D] = hi
            wq[pl.ds(pl.multiple_of(i * 16 + D, 16), 16), part * D:(part + 1) * D] = hi
            wq[pl.ds(pl.multiple_of(i * 16 + 2 * D, 16), 16), part * D:(part + 1) * D] = lo
        return 0

    lax.fori_loop(0, D // 16, split_q, 0)
    copy_o.wait()

    def split_o(i, _):
        r = pl.ds(pl.multiple_of(i * 16, 16), 16)
        hi, lo = hi_lo(stage_o[r, :])
        wo[r, :] = hi
        wo[pl.ds(pl.multiple_of(i * 16 + D, 16), 16), :] = hi
        wo[pl.ds(pl.multiple_of(i * 16 + 2 * D, 16), 16), :] = lo
        return 0

    lax.fori_loop(0, D // 16, split_o, 0)

    for t in range(6):
        cols = slice(t * 256, (t + 1) * 256)
        qkv[:, cols] = dot(xcat[...], wq[0:2 * D, cols]) + dot(xcat[:, 0:D], wq[2 * D:3 * D, cols])

    lat_at = lax.axis_index("lat")
    q_at = lax.broadcasted_iota(jnp.int32, (TOK_PAD, 128), 0)
    k_at = lax.broadcasted_iota(jnp.int32, (TOK_PAD, 128), 1)
    q_cell = jnp.where(q_at >= CELL_PAD, q_at - CELL_PAD, q_at)
    k_cell = jnp.where(k_at >= CELL_PAD, k_at - CELL_PAD, k_at)
    k_real = (k_cell < CELLS)
    for j, (b, _) in enumerate(runs):
        copies_b[j].wait()
        bias_v[j, 1600:, :] = jnp.zeros((bias_v.shape[1] - 1600, 100), F32)
        idq = jnp.zeros((TOK_PAD, 128), jnp.int32)
        idk = jnp.zeros((TOK_PAD, 128), jnp.int32)
        for i in range(WLAT):
            at = lat_at * ROWS + b * WLAT + i + HALF_LAT
            one = ids_ref[jnp.where(at >= 240, at - 240, at)]
            idq = jnp.where(q_cell >= i * WLON, one, idq)
            idk = jnp.where(k_cell >= i * WLON, one, idk)
        ok = jnp.logical_and(idq == idk, k_real)
        early = k_at < CELL_PAD
        for h in range(HEADS):
            raw = jnp.concatenate(
                [bias_v[j, pl.ds(h, CELL_PAD, stride=HEADS), :],
                 bias_v[j, pl.ds(h + CELLS * HEADS, CELL_PAD, stride=HEADS), :]], axis=0) * LOG2E
            raw = jnp.concatenate([raw, jnp.zeros((TOK_PAD, 28), F32)], axis=1)
            moved = pltpu.roll(raw, CELL_PAD - CELLS, 1)
            biasm[j, h] = jnp.where(ok, jnp.where(early, raw, moved), NEG)

    lane = lax.broadcasted_iota(jnp.int32, (TOK_PAD, 128), 1)
    low_half = lane < 64
    zeros16 = jnp.zeros((16, 256), BF)
    ends = []
    total = 0
    for _, ws in runs:
        total += len(ws)
        ends.append(total)

    def swap(x):
        return jnp.concatenate([x[:, 64:], x[:, :64]], axis=1)

    def attend_window(i, _):
        r = pl.ds(pl.multiple_of(i * TOK_PAD, TOK_PAD), TOK_PAD)
        slot = 0
        for e in ends[:-1]:
            slot = slot + jnp.where(i >= e, 1, 0)
        for g in range(4):
            q = qkv[r, g * 128:(g + 1) * 128]
            k = qkv[r, D + g * 128:D + (g + 1) * 128]
            v = qkv[r, 2 * D + g * 128:2 * D + (g + 1) * 128]
            qh = q.astype(BF).astype(F32)
            ql = q - qh
            rql = pltpu.roll(ql, 64, 1)
            kh = k.astype(BF).astype(F32)
            kl = k - kh
            rkh = pltpu.roll(kh, 64, 1)
            rkl = pltpu.roll(kl, 64, 1)
            vh, vl = hi_lo(v)
            vh = vh.astype(F32)
            vl = vl.astype(F32)
            sides_q = (jnp.where(low_half, qh, rql).astype(BF), jnp.where(low_half, rql, qh).astype(BF))
            sides_kh = (jnp.where(low_half, kh, rkh), jnp.where(low_half, rkh, kh))
            sides_kl = (jnp.where(low_half, kl, rkl), jnp.where(low_half, rkl, kl))
            his, los, inv, rhs = [], [], [], []
            for s in range(2):
                lhs = jnp.concatenate([sides_q[s], sides_q[s]], axis=1)
                keys = []
                for t in range(2):
                    own = jnp.logical_and((lane & 63) >= 32 * t, (lane & 63) < 32 * (t + 1))
                    part = jnp.concatenate(
                        [jnp.where(own, sides_kh[s], 0.0).astype(BF),
                         jnp.where(own, sides_kl[s], 0.0).astype(BF)], axis=1)
                    keys += [part, zeros16]
                scores = dot_t(lhs, jnp.concatenate(keys, axis=0))
                for t in range(2):
                    h = g * 4 + s * 2 + t
                    x = scores[:, t * 128:(t + 1) * 128] + biasm[slot, h]
                    x = jnp.exp2(x - jnp.max(x, axis=1, keepdims=True))
                    inv.append(1.0 / jnp.sum(x, axis=1, keepdims=True))
                    hi, lo = hi_lo(x)
                    his.append(hi)
                    los.append(lo)
                    own = jnp.logical_and(lane >= 32 * (2 * s + t), lane < 32 * (2 * s + t + 1))
                    part = jnp.concatenate(
                        [jnp.where(own, vh, 0.0).astype(BF), jnp.where(own, vl, 0.0).astype(BF)], axis=1)
                    rhs += [part, zeros16]
            lhs = jnp.concatenate([jnp.concatenate(his, axis=1), jnp.concatenate(los, axis=1)], axis=0)
            both = dot(lhs, jnp.concatenate(rhs, axis=0))
            both = both[:TOK_PAD] + both[TOK_PAD:]
            out = both[:, :128] + both[:, 128:]
            scale = jnp.where(
                lane < 64, jnp.where(lane < 32, inv[0], inv[1]), jnp.where(lane < 96, inv[2], inv[3]))
            hi, lo = hi_lo(out * scale)
            hcat[r, g * 128:(g + 1) * 128] = hi
            hcat[r, D + g * 128:D + (g + 1) * 128] = lo
        return 0

    lax.fori_loop(0, nw, attend_window, 0)

    for t in range(2):
        cols = slice(t * 256, (t + 1) * 256)
        qkv[:, cols] = dot(hcat[...], wo[0:2 * D, cols]) + dot(hcat[:, 0:D], wo[2 * D:3 * D, cols])

    def add_window(i, _):
        base = pl.multiple_of(i * SLAB, SLAB)
        for lev in range(2):
            r = pl.ds(pl.multiple_of(i * TOK_PAD + lev * CELL_PAD, CELL_PAD), CELL_PAD)
            for g in range(4):
                at = pl.ds(base + g * 2 + lev, CELL_PAD, stride=SUB)
                tok[at, :] = tok[at, :] + qkv[r, g * 128:(g + 1) * 128]
        return 0

    lax.fori_loop(0, nw, add_window, 0)
    for i in range(nw):
        move(i, dsts, False, sem_out.at[i])
    for i in range(nw):
        pltpu.make_async_copy(
            tok.at[pl.ds(i * SLAB, CELLS * SUB)], tok_hbm.at[pl.ds(0, CELLS * SUB)], sem_out.at[i]).wait()


def group_call(runs, ids, tok, halos, gain, shift, w_qkv, w_out, bias, out_so_far, name):
    nw = sum(len(ws) for _, ws in runs)
    nb = len(runs)
    halo = halos is not None
    aliased = out_so_far is not None
    any_spec = pl.BlockSpec(memory_space=pl.ANY)
    vmem_spec = pl.BlockSpec(memory_space=pltpu.VMEM)
    smem_spec = pl.BlockSpec(memory_space=pltpu.SMEM)
    args = [ids, tok]
    specs = [smem_spec, any_spec]
    if halo:
        args += list(halos)
        specs += [any_spec] * 3
    args += [gain, shift, w_qkv, w_out, bias]
    specs += [vmem_spec, vmem_spec, any_spec, any_spec, any_spec]
    aliases = {}
    if aliased:
        aliases = {len(args): 0}
        args.append(out_so_far)
        specs.append(any_spec)
    out_shapes = [jax.ShapeDtypeStruct(tok.shape, F32)]
    if halo:
        out_shapes += [jax.ShapeDtypeStruct(h.shape, F32) for h in halos]
    rows_all = nw * TOK_PAD
    return pl.pallas_call(
        functools.partial(group_kernel, runs, halo, aliased),
        out_shape=out_shapes,
        in_specs=specs,
        out_specs=[any_spec] * len(out_shapes),
        input_output_aliases=aliases,
        scratch_shapes=[
            pltpu.VMEM((nw * SLAB, 128), F32),
            pltpu.VMEM((D, 3 * D), F32),
            pltpu.VMEM((D, D), F32),
            pltpu.VMEM((nb, 1712, 100), F32),
            pltpu.VMEM((3 * D, 3 * D), BF),
            pltpu.VMEM((3 * D, D), BF),
            pltpu.VMEM((rows_all, 2 * D), BF),
            pltpu.VMEM((rows_all, 3 * D), F32),
            pltpu.VMEM((rows_all, 2 * D), BF),
            pltpu.VMEM((nb, HEADS, TOK_PAD, 128), F32),
            pltpu.SemaphoreType.DMA((nw,)),
            pltpu.SemaphoreType.DMA((2,)),
            pltpu.SemaphoreType.DMA((nb,)),
            pltpu.SemaphoreType.DMA((nw,)),
        ],
        compiler_params=pltpu.CompilerParams(vmem_limit_bytes=56 << 20),
        cost_estimate=pl.CostEstimate(
            flops=nw * 10**9, bytes_accessed=8 << 20, transcendentals=nw * 200000),
        name=name,
    )(*args)


def merge_kernel(s_ref, e_ref, c_ref, _, out_ref, sem):
    copies = []
    for row in range(HALF_LAT):
        copies.append((s_ref, row * S_COLS, row * COLS + HALF_LON, S_COLS))
        copies.append((c_ref, row * HALF_LON, row * COLS, HALF_LON))
    for row in range(HALF_LAT, ROWS):
        copies.append((e_ref, (row - HALF_LAT) * HALF_LON, row * COLS, HALF_LON))
    started = []
    for n, (src, start, place, count) in enumerate(copies):
        c = pltpu.make_async_copy(
            src.at[pl.ds(start * SUB, count * SUB)], out_ref.at[pl.ds(place * SUB, count * SUB)], sem.at[n])
        c.start()
        started.append(c)
    for c in started:
        c.wait()


def merge_call(s, e, c, out_so_far):
    any_spec = pl.BlockSpec(memory_space=pl.ANY)
    return pl.pallas_call(
        merge_kernel,
        out_shape=jax.ShapeDtypeStruct(out_so_far.shape, F32),
        in_specs=[pl.BlockSpec(memory_space=pltpu.VMEM)] * 3 + [any_spec],
        out_specs=any_spec,
        input_output_aliases={3: 0},
        scratch_shapes=[pltpu.SemaphoreType.DMA((HALF_LAT + ROWS,))],
        name="merge",
    )(s, e, c, out_so_far)


def shift_pairs(dlon, dlat):
    n_lon, n_lat = lax.axis_size("lon"), lax.axis_size("lat")
    pairs = []
    for lon in range(n_lon):
        for lat in range(n_lat):
            to = ((lon + dlon) % n_lon) * n_lat + (lat + dlat) % n_lat
            pairs.append((lon * n_lat + lat, to))
    return pairs


def send(value, dlon, dlat):
    return lax.ppermute(value, ("lon", "lat"), shift_pairs(dlon, dlat))


def body(tokens, ln_gain, ln_shift, w_qkv, w_out, region_ids, position_bias):
    tok = tokens.transpose(1, 2, 0, 3).reshape(ROWS, COLS, 2, 4, 128)
    tok = tok.transpose(0, 1, 3, 2, 4).reshape(ROWS, COLS * SUB, 128)
    bias = position_bias.transpose(0, 2, 1, 3).reshape(BANDS * 100 * HEADS, 100)
    edge = HALF_LON * SUB
    s = send(tok[:HALF_LAT, edge:].reshape(-1, 128), 0, -1)
    e = send(tok[HALF_LAT:, :edge].reshape(-1, 128), -1, 0)
    c = send(tok[:HALF_LAT, :edge].reshape(-1, 128), -1, -1)
    tok = tok.reshape(-1, 128)
    common = (ln_gain, ln_shift, w_qkv, w_out, bias)
    inner = tuple(range(ACROSS - 1))
    (out,) = group_call(((0, inner),), region_ids, tok, None, *common, None, "band0")
    out, s, e, c = group_call(
        ((2, tuple(range(ACROSS))), (0, (ACROSS - 1,)), (1, (ACROSS - 1,))),
        region_ids, tok, (s, e, c), *common, out, "rim")
    s = send(s, 0, 1)
    e = send(e, 1, 0)
    c = send(c, 1, 1)
    (out,) = group_call(((1, inner),), region_ids, tok, None, *common, out, "band1")
    out = merge_call(s, e, c, out)
    out = out.reshape(ROWS, COLS, 4, 2, 128).transpose(0, 1, 3, 2, 4).reshape(ROWS, COLS, 2, D)
    return out.transpose(2, 0, 1, 3)


def solution(mesh):
    in_specs = (P(None, "lat", "lon", None), P(), P(), P(), P(), P(), P("lat", None, None, None))
    out_specs = P(None, "lat", "lon", None)
    return jax.shard_map(body, mesh=mesh, in_specs=in_specs, out_specs=out_specs, check_vma=False)
```

```python
import functools
import math

import jax
import jax.numpy as jnp
from jax import lax
from jax.experimental import pallas as pl
from jax.experimental.pallas import tpu as pltpu
from jax.sharding import PartitionSpec as P

D = 512
HEADS = 16
WLON = 10
WLAT = 5
HALF_LAT = WLAT // 2
HALF_LON = WLON // 2
ROWS = 15
COLS = 100
BANDS = ROWS // WLAT
ACROSS = COLS // WLON
SUB = 8
CELLS = WLAT * WLON
CELL_PAD = 56
TOK_PAD = 2 * CELL_PAD
WIN_ROWS = WLAT + 1
SLAB = WIN_ROWS * WLON * SUB
S_COLS = COLS - HALF_LON
NEG = -1e30
LOG2E = math.log2(math.e)
TILES = 3
QSCALE = LOG2E / math.sqrt(D // HEADS)
BF = jnp.bfloat16
F32 = jnp.float32


def hi_lo(x):
    hi = x.astype(BF)
    lo = (x - hi.astype(F32)).astype(BF)
    return hi, lo


def pieces(band, win):
    top = WLAT * band + HALF_LAT
    col = WLON * win + HALF_LON
    north = min(WLAT, ROWS - top)
    wide = min(WLON, COLS - col)
    out = [(0, 0, "t", top, col, north, wide)]
    if north < WLAT:
        out.append((north, 0, "s", 0, col - HALF_LON, WLAT - north, wide))
    if wide < WLON:
        out.append((0, wide, "e", top - HALF_LAT, 0, north, WLON - wide))
        if north < WLAT:
            out.append((north, wide, "c", 0, 0, WLAT - north, WLON - wide))
    return out


def dot(a, b):
    return lax.dot_general(a, b, (((1,), (0,)), ((), ())), preferred_element_type=F32)


def dot_t(a, b):
    return lax.dot_general(a, b, (((1,), (1,)), ((), ())), preferred_element_type=F32)


def group_kernel(runs, halo, aliased, first, *refs):
    refs = list(refs)
    ids_ref, tok_hbm = refs[:2]
    del refs[:2]
    srcs = {"t": tok_hbm}
    if halo:
        srcs.update(zip("sec", refs[:3]))
        del refs[:3]
    gain_ref, shift_ref, wqkv_hbm, wout_hbm, bias_hbm = refs[:5]
    del refs[:5]
    if aliased:
        del refs[0]
    dsts = {"t": refs.pop(0)}
    if halo:
        dsts.update(zip("sec", refs[:3]))
        del refs[:3]
    if first:
        wq_out, wo_out = refs[:2]
        stage_q, stage_o = refs[-2:]
        refs = refs[2:-2]
    (tok3, bias_v, wq, wo, xcat, qkv, q_t, v_t, hcat, biasm, sem_tok, sem_w, sem_b, sem_out) = refs
    tok = tok3.reshape(tok3.shape[0] * WLON * SUB, 128)

    wins = [(b, w) for b, ws in runs for w in ws]
    nw = len(wins)
    rows_all = nw * TOK_PAD

    def move(i, others, into, sem):
        band, win = wins[i]
        for r0, c0, name, row, col, rows, cols in pieces(band, win):
            here = tok3.at[pl.ds(i * WIN_ROWS + r0, rows), pl.ds(c0 * SUB, cols * SUB)]
            there = others[name].at[pl.ds(row, rows), pl.ds(col * SUB, cols * SUB)]
            if into:
                pltpu.make_async_copy(there, here, sem).start()
            else:
                pltpu.make_async_copy(here, there, sem).start()

    def whole(i, others):
        return others["t"].at[pl.ds(0, WLAT), pl.ds(0, WLON * SUB)], tok3.at[
            pl.ds(i * WIN_ROWS, WLAT), pl.ds(0, WLON * SUB)]

    land_q, land_o = (stage_q, stage_o) if first else (wq, wo)
    copies_q = []
    for t in range(TILES):
        cols = pl.ds(t * D, D)
        copies_q.append(pltpu.make_async_copy(wqkv_hbm.at[:, cols], land_q.at[:, cols], sem_w.at[t]))
    copy_o = pltpu.make_async_copy(wout_hbm, land_o, sem_w.at[TILES])
    copies_b = []
    for j, (b, _) in enumerate(runs):
        copies_b.append(pltpu.make_async_copy(
            bias_hbm.at[pl.ds(b * 1600, 1600)], bias_v.at[j, pl.ds(0, 1600)], sem_b.at[j]))
    for i in range(nw):
        move(i, srcs, True, sem_tok.at[i])
    for c in [copies_q[2], copies_q[0]] + copies_b + [copies_q[1], copy_o]:
        c.start()

    gain = gain_ref[...].reshape(1, D)
    shift = shift_ref[...].reshape(1, D)
    pad_rows = jnp.zeros(((CELL_PAD - CELLS) * SUB, 128), F32)

    def norm_window(i, _):
        base = pl.multiple_of(i * SLAB, SLAB)
        there, here = whole(i, srcs)
        pltpu.make_async_copy(there, here, sem_tok.at[i]).wait()
        tok[pl.ds(base + CELLS * SUB, (CELL_PAD - CELLS) * SUB), :] = pad_rows
        parts = [
            jnp.concatenate(
                [tok[pl.ds(base + g * 2 + lev, CELL_PAD, stride=SUB), :] for lev in range(2)], axis=0)
            for g in range(4)
        ]
        center = jnp.sum(parts[0] + parts[1] + parts[2] + parts[3], axis=1, keepdims=True) * (1.0 / D)
        parts = [p - center for p in parts]
        sq = [p * p for p in parts]
        spread = jnp.sum(sq[0] + sq[1] + sq[2] + sq[3], axis=1, keepdims=True) * (1.0 / D)
        scale = lax.rsqrt(spread + 1e-05)
        r = pl.ds(pl.multiple_of(i * TOK_PAD, TOK_PAD), TOK_PAD)
        for g in range(4):
            cols = slice(g * 128, (g + 1) * 128)
            y = parts[g] * scale * gain[:, cols] + shift[:, cols]
            hi, lo = hi_lo(y)
            xcat[r, g * 128:(g + 1) * 128] = hi
            xcat[r, D + g * 128:D + (g + 1) * 128] = lo
        return 0

    lax.fori_loop(0, nw, norm_window, 0)

    def split_q(t):
        cols = slice(t * D, (t + 1) * D)
        x = stage_q[:, cols]
        if t == 0:
            x = x * QSCALE
        hi, lo = hi_lo(x)
        wq[:D, cols] = hi
        wq[D:, cols] = lo

    def project(t):
        cols = slice(t * D, (t + 1) * D)
        qkv[:, cols] = (dot(xcat[:, :D], wq[:D, cols]) + dot(xcat[:, D:], wq[:D, cols])
                        + dot(xcat[:, :D], wq[D:, cols]))

    pad16 = jnp.zeros((128 - TOK_PAD, 128), F32)

    def turn(t, out):
        for i in range(nw):
            for g in range(4):
                x = qkv[i * TOK_PAD:(i + 1) * TOK_PAD, t * D + g * 128:t * D + (g + 1) * 128]
                hi, lo = hi_lo(jnp.concatenate([x, pad16], axis=0).T)
                top = i * 2 * D + g * 128
                out[top:top + 128, :] = hi
                out[top + D:top + D + 128, :] = lo

    copies_q[2].wait()
    if first:
        split_q(2)
    copies_q[0].wait()
    if first:
        split_q(0)
    project(2)
    for c in copies_b:
        c.wait()
    copies_q[1].wait()
    if first:
        split_q(1)
        copy_o.wait()
        hi, lo = hi_lo(stage_o[...])
        wo[:D, :] = hi
        wo[D:, :] = lo
    project(0)
    turn(2, v_t)
    project(1)
    turn(0, q_t)

    lat_at = lax.axis_index("lat")
    k_at = lax.broadcasted_iota(jnp.int32, (TOK_PAD, 128), 0)
    q_at = lax.broadcasted_iota(jnp.int32, (TOK_PAD, 128), 1)
    q_cell = jnp.where(q_at >= CELL_PAD, q_at - CELL_PAD, q_at)
    k_cell = jnp.where(k_at >= CELL_PAD, k_at - CELL_PAD, k_at)
    lane = lax.broadcasted_iota(jnp.int32, (TOK_PAD, 128), 1)
    for j, (b, _) in enumerate(runs):
        bias_v[j, 1600:, :] = jnp.zeros((bias_v.shape[1] - 1600, 100), F32)
        idq = jnp.zeros((TOK_PAD, 128), jnp.int32)
        idk = jnp.zeros((TOK_PAD, 128), jnp.int32)
        for i in range(WLAT):
            at = lat_at * ROWS + b * WLAT + i + HALF_LAT
            one = ids_ref[jnp.where(at >= 240, at - 240, at)]
            idq = jnp.where(q_cell >= i * WLON, one, idq)
            idk = jnp.where(k_cell >= i * WLON, one, idk)
        ok = jnp.logical_and(idq == idk, k_cell < CELLS)
        for h in range(HEADS):
            raw = jnp.concatenate(
                [bias_v[j, pl.ds(h, CELL_PAD, stride=HEADS), :],
                 bias_v[j, pl.ds(h + CELLS * HEADS, CELL_PAD, stride=HEADS), :],
                 jnp.zeros((128 - TOK_PAD, 100), F32)], axis=0) * LOG2E
            raw = jnp.concatenate([raw, jnp.zeros((128, 28), F32)], axis=1)
            moved = pltpu.roll(raw, CELL_PAD - CELLS, 1)
            wide = lax.broadcasted_iota(jnp.int32, (128, 128), 1)
            full = jnp.where(wide < CELL_PAD, raw, moved).T
            biasm[j, h] = jnp.where(ok, full[:TOK_PAD], NEG)

    if first:
        keep_q = pltpu.make_async_copy(wq, wq_out, sem_w.at[0])
        keep_q.start()
        keep_o = pltpu.make_async_copy(wo, wo_out, sem_w.at[1])
        keep_o.start()

    low_half = lane < 64
    blank = jnp.zeros((32, 128), BF)
    ends = []
    total = 0
    for _, ws in runs:
        total += len(ws)
        ends.append(total)

    def attend_window(i, _):
        r = pl.ds(pl.multiple_of(i * TOK_PAD, TOK_PAD), TOK_PAD)
        base = pl.multiple_of(i * 2 * D, 2 * D)
        slot = 0
        for e in ends[:-1]:
            slot = slot + jnp.where(i >= e, 1, 0)
        for g in range(4):
            k = qkv[r, D + g * 128:D + (g + 1) * 128]
            kh, kl = hi_lo(k)
            rkh = pltpu.roll(kh, 64, 1)
            rkl = pltpu.roll(kl, 64, 1)
            lhs_pairs = (
                jnp.concatenate([jnp.where(low_half, kh, rkl), kh[:, :64]], axis=1),
                jnp.concatenate([jnp.where(low_half, rkh, kl), rkh[:, :64]], axis=1),
            )
            outs = []
            for s in range(2):
                rows = []
                for part in (0, 0, D):
                    at = part + g * 128 + 64 * s
                    rows.append(jnp.concatenate([q_t[pl.ds(base + at, 32), :], blank], axis=1))
                    rows.append(jnp.concatenate([blank, q_t[pl.ds(base + at + 32, 32), :]], axis=1))
                scores = dot(lhs_pairs[s], jnp.concatenate(rows, axis=0))
                for t in range(2):
                    h = 2 * s + t
                    x = scores[:, t * 128:(t + 1) * 128] + biasm[slot, g * 4 + h]
                    x = jnp.exp2(x - jnp.max(x, axis=0, keepdims=True))
                    inv = 1.0 / jnp.sum(x, axis=0, keepdims=True)
                    hi, lo = hi_lo(x)
                    at = base + g * 128 + 32 * h
                    vals = jnp.concatenate([v_t[pl.ds(at, 32), :], v_t[pl.ds(at + D, 32), :]], axis=0)
                    both = dot(vals[:, :TOK_PAD], jnp.concatenate([hi, lo], axis=1))
                    both = both[:, :128] + both[:, 128:]
                    outs.append((both[:32] + both[32:]) * inv)
            hi, lo = hi_lo(jnp.concatenate(outs, axis=0).T[:TOK_PAD])
            hcat[r, g * 128:(g + 1) * 128] = hi
            hcat[r, D + g * 128:D + (g + 1) * 128] = lo
        return 0

    lax.fori_loop(0, nw, attend_window, 0, unroll=3)

    if not first:
        copy_o.wait()
    for t in range(2):
        cols = slice(t * 256, (t + 1) * 256)
        proj = (dot(hcat[:, :D], wo[:D, cols]) + dot(hcat[:, D:], wo[:D, cols])
                + dot(hcat[:, :D], wo[D:, cols]))
        for i in range(nw):
            for lev in range(2):
                top = i * TOK_PAD + lev * CELL_PAD
                for g in range(2):
                    at = pl.ds(i * SLAB + (2 * t + g) * 2 + lev, CELL_PAD, stride=SUB)
                    tok[at, :] = tok[at, :] + proj[top:top + CELL_PAD, g * 128:(g + 1) * 128]
    for i in range(nw):
        move(i, dsts, False, sem_out.at[i])
    if first:
        keep_q.wait()
        keep_o.wait()
    for i in range(nw):
        there, here = whole(i, dsts)
        pltpu.make_async_copy(here, there, sem_out.at[i]).wait()


def group_call(runs, ids, tok, halos, gain, shift, w_qkv, w_out, bias, out_so_far, name):
    nw = sum(len(ws) for _, ws in runs)
    nb = len(runs)
    halo = halos is not None
    aliased = out_so_far is not None
    first = w_qkv.dtype == F32
    any_spec = pl.BlockSpec(memory_space=pl.ANY)
    hbm_spec = pl.BlockSpec(memory_space=pltpu.HBM)
    vmem_spec = pl.BlockSpec(memory_space=pltpu.VMEM)
    smem_spec = pl.BlockSpec(memory_space=pltpu.SMEM)
    args = [ids, tok]
    specs = [smem_spec, hbm_spec]
    if halo:
        args += list(halos)
        specs += [any_spec] * 3
    args += [gain, shift, w_qkv, w_out, bias]
    specs += [vmem_spec, vmem_spec, hbm_spec, hbm_spec, hbm_spec]
    aliases = {}
    if aliased:
        aliases = {len(args): 0}
        args.append(out_so_far)
        specs.append(hbm_spec)
    out_shapes = [jax.ShapeDtypeStruct(tok.shape, F32)]
    if halo:
        out_shapes += [jax.ShapeDtypeStruct(h.shape, F32) for h in halos]
    if first:
        out_shapes += [jax.ShapeDtypeStruct((2 * D, 3 * D), BF), jax.ShapeDtypeStruct((2 * D, D), BF)]
    stages = [pltpu.VMEM((D, 3 * D), F32), pltpu.VMEM((D, D), F32)] if first else []
    rows_all = nw * TOK_PAD
    return pl.pallas_call(
        functools.partial(group_kernel, runs, halo, aliased, first),
        out_shape=out_shapes,
        in_specs=specs,
        out_specs=[hbm_spec] * len(out_shapes),
        input_output_aliases=aliases,
        scratch_shapes=[
            pltpu.VMEM((nw * WIN_ROWS, WLON * SUB, 128), F32),
            pltpu.VMEM((nb, 1712, 100), F32),
            pltpu.VMEM((2 * D, 3 * D), BF),
            pltpu.VMEM((2 * D, D), BF),
            pltpu.VMEM((rows_all, 2 * D), BF),
            pltpu.VMEM((rows_all, 3 * D), F32),
            pltpu.VMEM((nw * 2 * D, 128), BF),
            pltpu.VMEM((nw * 2 * D, 128), BF),
            pltpu.VMEM((rows_all, 2 * D), BF),
            pltpu.VMEM((nb, HEADS, TOK_PAD, 128), F32),
            pltpu.SemaphoreType.DMA((nw,)),
            pltpu.SemaphoreType.DMA((TILES + 1,)),
            pltpu.SemaphoreType.DMA((nb,)),
            pltpu.SemaphoreType.DMA((nw,)),
        ] + stages,
        compiler_params=pltpu.CompilerParams(vmem_limit_bytes=(52 if halo else 56) << 20),
        cost_estimate=pl.CostEstimate(
            flops=nw * 10**9, bytes_accessed=8 << 20, transcendentals=nw * 200000),
        name=name,
    )(*args)


def rim_parts(whole_ref, s_ref, e_ref, c_ref):
    edge = HALF_LON * SUB
    return (
        (s_ref, whole_ref.at[pl.ds(0, HALF_LAT), pl.ds(edge, S_COLS * SUB)]),
        (e_ref, whole_ref.at[pl.ds(HALF_LAT, ROWS - HALF_LAT), pl.ds(0, edge)]),
        (c_ref, whole_ref.at[pl.ds(0, HALF_LAT), pl.ds(0, edge)]),
    )


def merge_kernel(s_ref, e_ref, c_ref, _, out_ref, sem):
    copies = [pltpu.make_async_copy(part, place, sem.at[n])
              for n, (part, place) in enumerate(rim_parts(out_ref, s_ref, e_ref, c_ref))]
    for c in copies:
        c.start()
    for c in copies:
        c.wait()


def pack_kernel(tok_ref, s_ref, e_ref, c_ref, sem):
    copies = [pltpu.make_async_copy(place, part, sem.at[n])
              for n, (part, place) in enumerate(rim_parts(tok_ref, s_ref, e_ref, c_ref))]
    for c in copies:
        c.start()
    for c in copies:
        c.wait()


def pack_call(tok):
    edge = HALF_LON * SUB
    return pl.pallas_call(
        pack_kernel,
        out_shape=[jax.ShapeDtypeStruct((HALF_LAT, S_COLS * SUB, 128), F32),
                   jax.ShapeDtypeStruct((ROWS - HALF_LAT, edge, 128), F32),
                   jax.ShapeDtypeStruct((HALF_LAT, edge, 128), F32)],
        in_specs=[pl.BlockSpec(memory_space=pltpu.HBM)],
        out_specs=[pl.BlockSpec(memory_space=pl.ANY)] * 3,
        scratch_shapes=[pltpu.SemaphoreType.DMA((3,))],
        compiler_params=pltpu.CompilerParams(vmem_limit_bytes=52 << 20),
        name="pack",
    )(tok)


def merge_call(s, e, c, out_so_far):
    any_spec = pl.BlockSpec(memory_space=pl.ANY)
    return pl.pallas_call(
        merge_kernel,
        out_shape=jax.ShapeDtypeStruct(out_so_far.shape, F32),
        in_specs=[any_spec] * 3 + [pl.BlockSpec(memory_space=pltpu.HBM)],
        out_specs=pl.BlockSpec(memory_space=pltpu.HBM),
        input_output_aliases={3: 0},
        scratch_shapes=[pltpu.SemaphoreType.DMA((3,))],
        compiler_params=pltpu.CompilerParams(vmem_limit_bytes=4 << 20),
        name="merge",
    )(s, e, c, out_so_far)


def shift_pairs(dlon, dlat):
    n_lon, n_lat = lax.axis_size("lon"), lax.axis_size("lat")
    pairs = []
    for lon in range(n_lon):
        for lat in range(n_lat):
            to = ((lon + dlon) % n_lon) * n_lat + (lat + dlat) % n_lat
            pairs.append((lon * n_lat + lat, to))
    return pairs


def send(value, dlon, dlat):
    return lax.ppermute(value, ("lon", "lat"), shift_pairs(dlon, dlat))


def body(tokens, ln_gain, ln_shift, w_qkv, w_out, region_ids, position_bias):
    tok = tokens.transpose(1, 2, 0, 3).reshape(ROWS, COLS, 2, 4, 128)
    tok = tok.transpose(0, 1, 3, 2, 4).reshape(ROWS, COLS * SUB, 128)
    bias = position_bias.transpose(0, 2, 1, 3).reshape(BANDS * 100 * HEADS, 100)
    s, e, c = pack_call(tok)
    s = send(s, 0, -1)
    e = send(e, -1, 0)
    c = send(c, -1, -1)
    common = (ln_gain, ln_shift, w_qkv, w_out, bias)
    inner = tuple(range(ACROSS - 1))
    out, wq, wo = group_call(((0, inner),), region_ids, tok, None, *common, None, "band0")
    common = (ln_gain, ln_shift, wq, wo, bias)
    out, s, e, c = group_call(
        ((2, tuple(range(ACROSS))), (0, (ACROSS - 1,)), (1, (ACROSS - 1,))),
        region_ids, tok, (s, e, c), *common, out, "rim")
    s = send(s, 0, 1)
    e = send(e, 1, 0)
    c = send(c, 1, 1)
    (out,) = group_call(((1, inner),), region_ids, tok, None, *common, out, "band1")
    out = merge_call(s, e, c, out)
    out = out.reshape(ROWS, COLS, 4, 2, 128).transpose(0, 1, 3, 2, 4).reshape(ROWS, COLS, 2, D)
    return out.transpose(2, 0, 1, 3)


def solution(mesh):
    in_specs = (P(None, "lat", "lon", None), P(), P(), P(), P(), P(), P("lat", None, None, None))
    out_specs = P(None, "lat", "lon", None)
    return jax.shard_map(body, mesh=mesh, in_specs=in_specs, out_specs=out_specs, check_vma=False)
```

```python
import functools
import math

import jax
import jax.numpy as jnp
from jax import lax
from jax.experimental import pallas as pl
from jax.experimental.pallas import tpu as pltpu
from jax.sharding import PartitionSpec as P

D = 512
HEADS = 16
WLON = 10
WLAT = 5
HALF_LAT = WLAT // 2
HALF_LON = WLON // 2
ROWS = 15
COLS = 100
BANDS = ROWS // WLAT
ACROSS = COLS // WLON
SUB = 8
CELLS = WLAT * WLON
CELL_PAD = 56
TOK_PAD = 2 * CELL_PAD
WIN_ROWS = WLAT + 1
SLAB = WIN_ROWS * WLON * SUB
S_COLS = COLS - HALF_LON
NEG = -1e30
LOG2E = math.log2(math.e)
TILES = 3
UNROLL = 3
AHEAD = 6
QSCALE = LOG2E / math.sqrt(D // HEADS)
BF = jnp.bfloat16
F32 = jnp.float32


def hi_lo(x):
    hi = x.astype(BF)
    lo = (x - hi.astype(F32)).astype(BF)
    return hi, lo


def pieces(band, win):
    top = WLAT * band + HALF_LAT
    col = WLON * win + HALF_LON
    north = min(WLAT, ROWS - top)
    wide = min(WLON, COLS - col)
    out = [(0, 0, "t", top, col, north, wide)]
    if north < WLAT:
        out.append((north, 0, "s", 0, col - HALF_LON, WLAT - north, wide))
    if wide < WLON:
        out.append((0, wide, "e", top - HALF_LAT, 0, north, WLON - wide))
        if north < WLAT:
            out.append((north, wide, "c", 0, 0, WLAT - north, WLON - wide))
    return out


def dot(a, b):
    return lax.dot_general(a, b, (((1,), (0,)), ((), ())), preferred_element_type=F32)


def dot_t(a, b):
    return lax.dot_general(a, b, (((1,), (1,)), ((), ())), preferred_element_type=F32)


def group_kernel(runs, halo, aliased, first, *refs):
    refs = list(refs)
    ids_ref, tok_hbm = refs[:2]
    del refs[:2]
    srcs = {"t": tok_hbm}
    if halo:
        srcs.update(zip("sec", refs[:3]))
        del refs[:3]
    gain_ref, shift_ref, wqkv_hbm, wout_hbm, bias_hbm = refs[:5]
    del refs[:5]
    if aliased:
        del refs[0]
    dsts = {"t": refs.pop(0)}
    if halo:
        dsts.update(zip("sec", refs[:3]))
        del refs[:3]
    if first:
        wq_out, wo_out = refs[:2]
        stage_q, stage_o = refs[-2:]
        refs = refs[2:-2]
    (tok3, bias_v, wq, wo, xcat, qkv, q_t, v_t, hcat, biasm, sem_tok, sem_w, sem_b, sem_out) = refs
    tok = tok3.reshape(tok3.shape[0] * WLON * SUB, 128)

    wins = [(b, w) for b, ws in runs for w in ws]
    nw = len(wins)
    rows_all = nw * TOK_PAD

    def move(i, others, into, sem):
        band, win = wins[i]
        for r0, c0, name, row, col, rows, cols in pieces(band, win):
            here = tok3.at[pl.ds(i * WIN_ROWS + r0, rows), pl.ds(c0 * SUB, cols * SUB)]
            there = others[name].at[pl.ds(row, rows), pl.ds(col * SUB, cols * SUB)]
            if into:
                pltpu.make_async_copy(there, here, sem).start()
            else:
                pltpu.make_async_copy(here, there, sem).start()

    def whole(i, others):
        return others["t"].at[pl.ds(0, WLAT), pl.ds(0, WLON * SUB)], tok3.at[
            pl.ds(i * WIN_ROWS, WLAT), pl.ds(0, WLON * SUB)]

    land_q, land_o = (stage_q, stage_o) if first else (wq, wo)
    copies_q = []
    for t in range(TILES):
        cols = pl.ds(t * D, D)
        copies_q.append(pltpu.make_async_copy(wqkv_hbm.at[:, cols], land_q.at[:, cols], sem_w.at[t]))
    copy_o = pltpu.make_async_copy(wout_hbm, land_o, sem_w.at[TILES])
    copies_b = []
    for j, (b, _) in enumerate(runs):
        copies_b.append(pltpu.make_async_copy(
            bias_hbm.at[pl.ds(b * 1600, 1600)], bias_v.at[j, pl.ds(0, 1600)], sem_b.at[j]))
    for i in range(nw):
        move(i, srcs, True, sem_tok.at[i])
    for c in [copies_q[2], copies_q[0]] + copies_b + [copies_q[1], copy_o]:
        c.start()

    gain = gain_ref[...].reshape(1, D)
    shift = shift_ref[...].reshape(1, D)
    pad_rows = jnp.zeros(((CELL_PAD - CELLS) * SUB, 128), F32)

    def norm_window(i, _):
        base = pl.multiple_of(i * SLAB, SLAB)
        there, here = whole(i, srcs)
        pltpu.make_async_copy(there, here, sem_tok.at[i]).wait()
        tok[pl.ds(base + CELLS * SUB, (CELL_PAD - CELLS) * SUB), :] = pad_rows
        parts = [
            jnp.concatenate(
                [tok[pl.ds(base + g * 2 + lev, CELL_PAD, stride=SUB), :] for lev in range(2)], axis=0)
            for g in range(4)
        ]
        center = jnp.sum(parts[0] + parts[1] + parts[2] + parts[3], axis=1, keepdims=True) * (1.0 / D)
        parts = [p - center for p in parts]
        sq = [p * p for p in parts]
        spread = jnp.sum(sq[0] + sq[1] + sq[2] + sq[3], axis=1, keepdims=True) * (1.0 / D)
        scale = lax.rsqrt(spread + 1e-05)
        r = pl.ds(pl.multiple_of(i * TOK_PAD, TOK_PAD), TOK_PAD)
        for g in range(4):
            cols = slice(g * 128, (g + 1) * 128)
            y = parts[g] * scale * gain[:, cols] + shift[:, cols]
            hi, lo = hi_lo(y)
            xcat[r, g * 128:(g + 1) * 128] = hi
            xcat[r, D + g * 128:D + (g + 1) * 128] = lo
        return 0

    lax.fori_loop(0, nw, norm_window, 0)

    def split_q(t):
        cols = slice(t * D, (t + 1) * D)
        x = stage_q[:, cols]
        if t == 0:
            x = x * QSCALE
        hi, lo = hi_lo(x)
        wq[:D, cols] = hi
        wq[D:, cols] = lo

    def project(t):
        cols = slice(t * D, (t + 1) * D)
        qkv[:, cols] = (dot(xcat[:, :D], wq[:D, cols]) + dot(xcat[:, D:], wq[:D, cols])
                        + dot(xcat[:, :D], wq[D:, cols]))

    pad16 = jnp.zeros((128 - TOK_PAD, 128), F32)

    def turn(t, out):
        for i in range(nw):
            for g in range(4):
                x = qkv[i * TOK_PAD:(i + 1) * TOK_PAD, t * D + g * 128:t * D + (g + 1) * 128]
                hi, lo = hi_lo(jnp.concatenate([x, pad16], axis=0).T)
                top = i * 2 * D + g * 128
                out[top:top + 128, :] = hi
                out[top + D:top + D + 128, :] = lo

    copies_q[2].wait()
    if first:
        split_q(2)
    copies_q[0].wait()
    if first:
        split_q(0)
    project(2)
    for c in copies_b:
        c.wait()
    copies_q[1].wait()
    if first:
        split_q(1)
        copy_o.wait()
        hi, lo = hi_lo(stage_o[...])
        wo[:D, :] = hi
        wo[D:, :] = lo
    project(0)
    turn(2, v_t)
    project(1)
    turn(0, q_t)

    lat_at = lax.axis_index("lat")
    k_at = lax.broadcasted_iota(jnp.int32, (TOK_PAD, 128), 0)
    q_at = lax.broadcasted_iota(jnp.int32, (TOK_PAD, 128), 1)
    q_cell = jnp.where(q_at >= CELL_PAD, q_at - CELL_PAD, q_at)
    k_cell = jnp.where(k_at >= CELL_PAD, k_at - CELL_PAD, k_at)
    lane = lax.broadcasted_iota(jnp.int32, (TOK_PAD, 128), 1)
    for j, (b, _) in enumerate(runs):
        bias_v[j, 1600:, :] = jnp.zeros((bias_v.shape[1] - 1600, 100), F32)
        idq = jnp.zeros((TOK_PAD, 128), jnp.int32)
        idk = jnp.zeros((TOK_PAD, 128), jnp.int32)
        for i in range(WLAT):
            at = lat_at * ROWS + b * WLAT + i + HALF_LAT
            one = ids_ref[jnp.where(at >= 240, at - 240, at)]
            idq = jnp.where(q_cell >= i * WLON, one, idq)
            idk = jnp.where(k_cell >= i * WLON, one, idk)
        ok = jnp.logical_and(idq == idk, k_cell < CELLS)
        for h in range(HEADS):
            raw = jnp.concatenate(
                [bias_v[j, pl.ds(h, CELL_PAD, stride=HEADS), :],
                 bias_v[j, pl.ds(h + CELLS * HEADS, CELL_PAD, stride=HEADS), :],
                 jnp.zeros((128 - TOK_PAD, 100), F32)], axis=0) * LOG2E
            raw = jnp.concatenate([raw, jnp.zeros((128, 28), F32)], axis=1)
            moved = pltpu.roll(raw, CELL_PAD - CELLS, 1)
            wide = lax.broadcasted_iota(jnp.int32, (128, 128), 1)
            full = jnp.where(wide < CELL_PAD, raw, moved).T
            biasm[j, h] = jnp.where(ok, full[:TOK_PAD], NEG)

    if first:
        keep_q = pltpu.make_async_copy(wq, wq_out, sem_w.at[0])
        keep_q.start()
        keep_o = pltpu.make_async_copy(wo, wo_out, sem_w.at[1])
        keep_o.start()

    low_half = lane < 64
    blank = jnp.zeros((32, 128), BF)
    ends = []
    total = 0
    for _, ws in runs:
        total += len(ws)
        ends.append(total)

    def attend_windows(step, _):
        items = [(u, g, s) for u in range(UNROLL) for g in range(4) for s in range(2)]
        keys, raw, outs = {}, {}, {}
        at_window = []
        for u in range(UNROLL):
            i = step * UNROLL + u
            slot = 0
            for e in ends[:-1]:
                slot = slot + jnp.where(i >= e, 1, 0)
            at_window.append((pl.ds(pl.multiple_of(i * TOK_PAD, TOK_PAD), TOK_PAD),
                              pl.multiple_of(i * 2 * D, 2 * D), slot))

        def score(u, g, s):
            r, base, _ = at_window[u]
            if s == 0:
                kh, kl = hi_lo(qkv[r, D + g * 128:D + (g + 1) * 128])
                rkh = pltpu.roll(kh, 64, 1)
                rkl = pltpu.roll(kl, 64, 1)
                keys[u, g] = (
                    jnp.concatenate([jnp.where(low_half, kh, rkl), kh[:, :64]], axis=1),
                    jnp.concatenate([jnp.where(low_half, rkh, kl), rkh[:, :64]], axis=1),
                )
            rows = []
            for part in (0, 0, D):
                at = base + part + g * 128 + 64 * s
                rows.append(jnp.concatenate([q_t[pl.ds(at, 32), :], blank], axis=1))
                rows.append(jnp.concatenate([blank, q_t[pl.ds(at + 32, 32), :]], axis=1))
            raw[u, g, s] = dot(keys[u, g][s], jnp.concatenate(rows, axis=0))

        def mix(u, g, s):
            r, base, slot = at_window[u]
            scores = raw.pop((u, g, s))
            for t in range(2):
                h = 2 * s + t
                x = scores[:, t * 128:(t + 1) * 128] + biasm[slot, g * 4 + h]
                x = jnp.exp2(x - jnp.max(x, axis=0, keepdims=True))
                inv = 1.0 / jnp.sum(x, axis=0, keepdims=True)
                hi, lo = hi_lo(x)
                at = base + g * 128 + 32 * h
                vals = jnp.concatenate([v_t[pl.ds(at, 32), :], v_t[pl.ds(at + D, 32), :]], axis=0)
                both = dot(vals[:, :TOK_PAD], jnp.concatenate([hi, lo], axis=1))
                both = both[:, :128] + both[:, 128:]
                outs.setdefault((u, g), []).append((both[:32] + both[32:]) * inv)
            if s == 1:
                hi, lo = hi_lo(jnp.concatenate(outs.pop((u, g)), axis=0).T[:TOK_PAD])
                hcat[r, g * 128:(g + 1) * 128] = hi
                hcat[r, D + g * 128:D + (g + 1) * 128] = lo

        for n in range(len(items) + AHEAD):
            if n < len(items):
                score(*items[n])
            if n >= AHEAD:
                mix(*items[n - AHEAD])
        return 0

    lax.fori_loop(0, nw // UNROLL, attend_windows, 0)

    if not first:
        copy_o.wait()
    for t in range(2):
        cols = slice(t * 256, (t + 1) * 256)
        proj = (dot(hcat[:, :D], wo[:D, cols]) + dot(hcat[:, D:], wo[:D, cols])
                + dot(hcat[:, :D], wo[D:, cols]))
        for i in range(nw):
            for lev in range(2):
                top = i * TOK_PAD + lev * CELL_PAD
                for g in range(2):
                    at = pl.ds(i * SLAB + (2 * t + g) * 2 + lev, CELL_PAD, stride=SUB)
                    tok[at, :] = tok[at, :] + proj[top:top + CELL_PAD, g * 128:(g + 1) * 128]
    for i in range(nw):
        move(i, dsts, False, sem_out.at[i])
    if first:
        keep_q.wait()
        keep_o.wait()
    for i in range(nw):
        there, here = whole(i, dsts)
        pltpu.make_async_copy(here, there, sem_out.at[i]).wait()


def group_call(runs, ids, tok, halos, gain, shift, w_qkv, w_out, bias, out_so_far, name):
    nw = sum(len(ws) for _, ws in runs)
    nb = len(runs)
    halo = halos is not None
    aliased = out_so_far is not None
    first = w_qkv.dtype == F32
    any_spec = pl.BlockSpec(memory_space=pl.ANY)
    hbm_spec = pl.BlockSpec(memory_space=pltpu.HBM)
    vmem_spec = pl.BlockSpec(memory_space=pltpu.VMEM)
    smem_spec = pl.BlockSpec(memory_space=pltpu.SMEM)
    args = [ids, tok]
    specs = [smem_spec, hbm_spec]
    if halo:
        args += list(halos)
        specs += [any_spec] * 3
    args += [gain, shift, w_qkv, w_out, bias]
    specs += [vmem_spec, vmem_spec, hbm_spec, hbm_spec, hbm_spec]
    aliases = {}
    if aliased:
        aliases = {len(args): 0}
        args.append(out_so_far)
        specs.append(hbm_spec)
    out_shapes = [jax.ShapeDtypeStruct(tok.shape, F32)]
    if halo:
        out_shapes += [jax.ShapeDtypeStruct(h.shape, F32) for h in halos]
    if first:
        out_shapes += [jax.ShapeDtypeStruct((2 * D, 3 * D), BF), jax.ShapeDtypeStruct((2 * D, D), BF)]
    stages = [pltpu.VMEM((D, 3 * D), F32), pltpu.VMEM((D, D), F32)] if first else []
    rows_all = nw * TOK_PAD
    return pl.pallas_call(
        functools.partial(group_kernel, runs, halo, aliased, first),
        out_shape=out_shapes,
        in_specs=specs,
        out_specs=[hbm_spec] * len(out_shapes),
        input_output_aliases=aliases,
        scratch_shapes=[
            pltpu.VMEM((nw * WIN_ROWS, WLON * SUB, 128), F32),
            pltpu.VMEM((nb, 1712, 100), F32),
            pltpu.VMEM((2 * D, 3 * D), BF),
            pltpu.VMEM((2 * D, D), BF),
            pltpu.VMEM((rows_all, 2 * D), BF),
            pltpu.VMEM((rows_all, 3 * D), F32),
            pltpu.VMEM((nw * 2 * D, 128), BF),
            pltpu.VMEM((nw * 2 * D, 128), BF),
            pltpu.VMEM((rows_all, 2 * D), BF),
            pltpu.VMEM((nb, HEADS, TOK_PAD, 128), F32),
            pltpu.SemaphoreType.DMA((nw,)),
            pltpu.SemaphoreType.DMA((TILES + 1,)),
            pltpu.SemaphoreType.DMA((nb,)),
            pltpu.SemaphoreType.DMA((nw,)),
        ] + stages,
        compiler_params=pltpu.CompilerParams(vmem_limit_bytes=(52 if halo else 56) << 20),
        cost_estimate=pl.CostEstimate(
            flops=nw * 10**9, bytes_accessed=8 << 20, transcendentals=nw * 200000),
        name=name,
    )(*args)


def rim_parts(whole_ref, s_ref, e_ref, c_ref):
    edge = HALF_LON * SUB
    return (
        (s_ref, whole_ref.at[pl.ds(0, HALF_LAT), pl.ds(edge, S_COLS * SUB)]),
        (e_ref, whole_ref.at[pl.ds(HALF_LAT, ROWS - HALF_LAT), pl.ds(0, edge)]),
        (c_ref, whole_ref.at[pl.ds(0, HALF_LAT), pl.ds(0, edge)]),
    )


def merge_kernel(s_ref, e_ref, c_ref, _, out_ref, sem):
    copies = [pltpu.make_async_copy(part, place, sem.at[n])
              for n, (part, place) in enumerate(rim_parts(out_ref, s_ref, e_ref, c_ref))]
    for c in copies:
        c.start()
    for c in copies:
        c.wait()


def pack_kernel(tok_ref, s_ref, e_ref, c_ref, sem):
    copies = [pltpu.make_async_copy(place, part, sem.at[n])
              for n, (part, place) in enumerate(rim_parts(tok_ref, s_ref, e_ref, c_ref))]
    for c in copies:
        c.start()
    for c in copies:
        c.wait()


def pack_call(tok):
    edge = HALF_LON * SUB
    return pl.pallas_call(
        pack_kernel,
        out_shape=[jax.ShapeDtypeStruct((HALF_LAT, S_COLS * SUB, 128), F32),
                   jax.ShapeDtypeStruct((ROWS - HALF_LAT, edge, 128), F32),
                   jax.ShapeDtypeStruct((HALF_LAT, edge, 128), F32)],
        in_specs=[pl.BlockSpec(memory_space=pltpu.HBM)],
        out_specs=[pl.BlockSpec(memory_space=pl.ANY)] * 3,
        scratch_shapes=[pltpu.SemaphoreType.DMA((3,))],
        compiler_params=pltpu.CompilerParams(vmem_limit_bytes=52 << 20),
        name="pack",
    )(tok)


def merge_call(s, e, c, out_so_far):
    any_spec = pl.BlockSpec(memory_space=pl.ANY)
    return pl.pallas_call(
        merge_kernel,
        out_shape=jax.ShapeDtypeStruct(out_so_far.shape, F32),
        in_specs=[any_spec] * 3 + [pl.BlockSpec(memory_space=pltpu.HBM)],
        out_specs=pl.BlockSpec(memory_space=pltpu.HBM),
        input_output_aliases={3: 0},
        scratch_shapes=[pltpu.SemaphoreType.DMA((3,))],
        compiler_params=pltpu.CompilerParams(vmem_limit_bytes=4 << 20),
        name="merge",
    )(s, e, c, out_so_far)


def shift_pairs(dlon, dlat):
    n_lon, n_lat = lax.axis_size("lon"), lax.axis_size("lat")
    pairs = []
    for lon in range(n_lon):
        for lat in range(n_lat):
            to = ((lon + dlon) % n_lon) * n_lat + (lat + dlat) % n_lat
            pairs.append((lon * n_lat + lat, to))
    return pairs


def send(value, dlon, dlat):
    return lax.ppermute(value, ("lon", "lat"), shift_pairs(dlon, dlat))


def body(tokens, ln_gain, ln_shift, w_qkv, w_out, region_ids, position_bias):
    tok = tokens.transpose(1, 2, 0, 3).reshape(ROWS, COLS, 2, 4, 128)
    tok = tok.transpose(0, 1, 3, 2, 4).reshape(ROWS, COLS * SUB, 128)
    bias = position_bias.transpose(0, 2, 1, 3).reshape(BANDS * 100 * HEADS, 100)
    s, e, c = pack_call(tok)
    s = send(s, 0, -1)
    e = send(e, -1, 0)
    c = send(c, -1, -1)
    common = (ln_gain, ln_shift, w_qkv, w_out, bias)
    inner = tuple(range(ACROSS - 1))
    out, wq, wo = group_call(((0, inner),), region_ids, tok, None, *common, None, "band0")
    common = (ln_gain, ln_shift, wq, wo, bias)
    out, s, e, c = group_call(
        ((2, tuple(range(ACROSS))), (0, (ACROSS - 1,)), (1, (ACROSS - 1,))),
        region_ids, tok, (s, e, c), *common, out, "rim")
    s = send(s, 0, 1)
    e = send(e, 1, 0)
    c = send(c, 1, 1)
    (out,) = group_call(((1, inner),), region_ids, tok, None, *common, out, "band1")
    out = merge_call(s, e, c, out)
    out = out.reshape(ROWS, COLS, 4, 2, 128).transpose(0, 1, 3, 2, 4).reshape(ROWS, COLS, 2, D)
    return out.transpose(2, 0, 1, 3)


def solution(mesh):
    in_specs = (P(None, "lat", "lon", None), P(), P(), P(), P(), P(), P("lat", None, None, None))
    out_specs = P(None, "lat", "lon", None)
    return jax.shard_map(body, mesh=mesh, in_specs=in_specs, out_specs=out_specs, check_vma=False)
```

```python
import functools
import math

import jax
import jax.numpy as jnp
from jax import lax
from jax.experimental import pallas as pl
from jax.experimental.pallas import tpu as pltpu
from jax.sharding import PartitionSpec as P

D = 512
HEADS = 16
WLON = 10
WLAT = 5
HALF_LAT = WLAT // 2
HALF_LON = WLON // 2
ROWS = 15
COLS = 100
BANDS = ROWS // WLAT
ACROSS = COLS // WLON
SUB = 8
CELLS = WLAT * WLON
CELL_PAD = 56
TOK_PAD = 2 * CELL_PAD
WIN_ROWS = WLAT + 1
SLAB = WIN_ROWS * WLON * SUB
S_COLS = COLS - HALF_LON
NEG = -1e30
LOG2E = math.log2(math.e)
TILES = 3
AHEAD = 8
QSCALE = LOG2E / math.sqrt(D // HEADS)
BF = jnp.bfloat16
F32 = jnp.float32


def hi_lo(x):
    hi = x.astype(BF)
    lo = (x - hi.astype(F32)).astype(BF)
    return hi, lo


def pieces(band, win):
    top = WLAT * band + HALF_LAT
    col = WLON * win + HALF_LON
    north = min(WLAT, ROWS - top)
    wide = min(WLON, COLS - col)
    out = [(0, 0, "t", top, col, north, wide)]
    if north < WLAT:
        out.append((north, 0, "s", 0, col - HALF_LON, WLAT - north, wide))
    if wide < WLON:
        out.append((0, wide, "e", top - HALF_LAT, 0, north, WLON - wide))
        if north < WLAT:
            out.append((north, wide, "c", 0, 0, WLAT - north, WLON - wide))
    return out


def dot(a, b):
    return lax.dot_general(a, b, (((1,), (0,)), ((), ())), preferred_element_type=F32)


def dot_t(a, b):
    return lax.dot_general(a, b, (((1,), (1,)), ((), ())), preferred_element_type=F32)


def group_kernel(runs, halo, aliased, first, *refs):
    refs = list(refs)
    ids_ref, tok_hbm = refs[:2]
    del refs[:2]
    srcs = {"t": tok_hbm}
    if halo:
        srcs.update(zip("sec", refs[:3]))
        del refs[:3]
    gain_ref, shift_ref, wqkv_hbm, wout_hbm, bias_hbm = refs[:5]
    del refs[:5]
    if aliased:
        del refs[0]
    dsts = {"t": refs.pop(0)}
    if halo:
        dsts.update(zip("sec", refs[:3]))
        del refs[:3]
    if first:
        wq_out, wo_out = refs[:2]
        stage_q, stage_o = refs[-2:]
        refs = refs[2:-2]
    (tok3, bias_v, wq, wo, xcat, qkv, q_t, v_t, hcat, biasm, sem_tok, sem_w, sem_b, sem_out) = refs
    tok = tok3.reshape(tok3.shape[0] * WLON * SUB, 128)

    wins = [(b, w) for b, ws in runs for w in ws]
    nw = len(wins)
    rows_all = nw * TOK_PAD

    def move(i, others, into, sem):
        band, win = wins[i]
        for r0, c0, name, row, col, rows, cols in pieces(band, win):
            here = tok3.at[pl.ds(i * WIN_ROWS + r0, rows), pl.ds(c0 * SUB, cols * SUB)]
            there = others[name].at[pl.ds(row, rows), pl.ds(col * SUB, cols * SUB)]
            if into:
                pltpu.make_async_copy(there, here, sem).start()
            else:
                pltpu.make_async_copy(here, there, sem).start()

    def whole(i, others):
        return others["t"].at[pl.ds(0, WLAT), pl.ds(0, WLON * SUB)], tok3.at[
            pl.ds(i * WIN_ROWS, WLAT), pl.ds(0, WLON * SUB)]

    land_q, land_o = (stage_q, stage_o) if first else (wq, wo)
    copies_q = []
    for t in range(TILES):
        cols = pl.ds(t * D, D)
        copies_q.append(pltpu.make_async_copy(wqkv_hbm.at[:, cols], land_q.at[:, cols], sem_w.at[t]))
    copy_o = pltpu.make_async_copy(wout_hbm, land_o, sem_w.at[TILES])
    copies_b = []
    for j, (b, _) in enumerate(runs):
        copies_b.append(pltpu.make_async_copy(
            bias_hbm.at[pl.ds(b * 1600, 1600)], bias_v.at[j, pl.ds(0, 1600)], sem_b.at[j]))
    for i in range(nw):
        move(i, srcs, True, sem_tok.at[i])
    for c in [copies_q[2], copies_q[0]] + copies_b + [copies_q[1], copy_o]:
        c.start()

    gain = gain_ref[...].reshape(1, D)
    shift = shift_ref[...].reshape(1, D)
    pad_rows = jnp.zeros(((CELL_PAD - CELLS) * SUB, 128), F32)

    def norm_window(i):
        base = pl.multiple_of(i * SLAB, SLAB)
        tok[pl.ds(base + CELLS * SUB, (CELL_PAD - CELLS) * SUB), :] = pad_rows
        parts = [
            jnp.concatenate(
                [tok[pl.ds(base + g * 2 + lev, CELL_PAD, stride=SUB), :] for lev in range(2)], axis=0)
            for g in range(4)
        ]
        center = jnp.sum(parts[0] + parts[1] + parts[2] + parts[3], axis=1, keepdims=True) * (1.0 / D)
        parts = [p - center for p in parts]
        sq = [p * p for p in parts]
        spread = jnp.sum(sq[0] + sq[1] + sq[2] + sq[3], axis=1, keepdims=True) * (1.0 / D)
        scale = lax.rsqrt(spread + 1e-05)
        r = pl.ds(pl.multiple_of(i * TOK_PAD, TOK_PAD), TOK_PAD)
        for g in range(4):
            cols = slice(g * 128, (g + 1) * 128)
            y = parts[g] * scale * gain[:, cols] + shift[:, cols]
            hi, lo = hi_lo(y)
            xcat[r, g * 128:(g + 1) * 128] = hi
            xcat[r, D + g * 128:D + (g + 1) * 128] = lo

    def norm_windows(step, _):
        for u in range(3):
            there, here = whole(step * 3 + u, srcs)
            pltpu.make_async_copy(there, here, sem_tok.at[step * 3 + u]).wait()
        for u in range(3):
            norm_window(step * 3 + u)
        return 0

    lax.fori_loop(0, nw // 3, norm_windows, 0)

    def split_q(t):
        cols = slice(t * D, (t + 1) * D)
        x = stage_q[:, cols]
        if t == 0:
            x = x * QSCALE
        hi, lo = hi_lo(x)
        wq[:D, cols] = hi
        wq[D:, cols] = lo

    def project(t):
        cols = slice(t * D, (t + 1) * D)
        qkv[:, cols] = (dot(xcat[:, :D], wq[:D, cols]) + dot(xcat[:, D:], wq[:D, cols])
                        + dot(xcat[:, :D], wq[D:, cols]))

    pad16 = jnp.zeros((128 - TOK_PAD, 128), F32)

    def turn(t, out):
        for i in range(nw):
            for g in range(4):
                x = qkv[i * TOK_PAD:(i + 1) * TOK_PAD, t * D + g * 128:t * D + (g + 1) * 128]
                hi, lo = hi_lo(jnp.concatenate([x, pad16], axis=0).T)
                top = i * 2 * D + g * 128
                out[top:top + 128, :] = hi
                out[top + D:top + D + 128, :] = lo

    copies_q[2].wait()
    if first:
        split_q(2)
    copies_q[0].wait()
    if first:
        split_q(0)
    project(2)
    for c in copies_b:
        c.wait()
    copies_q[1].wait()
    if first:
        split_q(1)
        copy_o.wait()
        hi, lo = hi_lo(stage_o[...])
        wo[:D, :] = hi
        wo[D:, :] = lo
    project(0)
    turn(2, v_t)
    project(1)
    turn(0, q_t)

    lat_at = lax.axis_index("lat")
    k_at = lax.broadcasted_iota(jnp.int32, (TOK_PAD, 128), 0)
    q_at = lax.broadcasted_iota(jnp.int32, (TOK_PAD, 128), 1)
    q_cell = jnp.where(q_at >= CELL_PAD, q_at - CELL_PAD, q_at)
    k_cell = jnp.where(k_at >= CELL_PAD, k_at - CELL_PAD, k_at)
    lane = lax.broadcasted_iota(jnp.int32, (TOK_PAD, 128), 1)
    for j, (b, _) in enumerate(runs):
        bias_v[j, 1600:, :] = jnp.zeros((bias_v.shape[1] - 1600, 100), F32)
        idq = jnp.zeros((TOK_PAD, 128), jnp.int32)
        idk = jnp.zeros((TOK_PAD, 128), jnp.int32)
        for i in range(WLAT):
            at = lat_at * ROWS + b * WLAT + i + HALF_LAT
            one = ids_ref[jnp.where(at >= 240, at - 240, at)]
            idq = jnp.where(q_cell >= i * WLON, one, idq)
            idk = jnp.where(k_cell >= i * WLON, one, idk)
        ok = jnp.logical_and(idq == idk, k_cell < CELLS)
        for h in range(HEADS):
            raw = jnp.concatenate(
                [bias_v[j, pl.ds(h, CELL_PAD, stride=HEADS), :],
                 bias_v[j, pl.ds(h + CELLS * HEADS, CELL_PAD, stride=HEADS), :],
                 jnp.zeros((128 - TOK_PAD, 100), F32)], axis=0) * LOG2E
            raw = jnp.concatenate([raw, jnp.zeros((128, 28), F32)], axis=1)
            moved = pltpu.roll(raw, CELL_PAD - CELLS, 1)
            wide = lax.broadcasted_iota(jnp.int32, (128, 128), 1)
            full = jnp.where(wide < CELL_PAD, raw, moved).T
            biasm[j, h] = jnp.where(ok, full[:TOK_PAD], NEG)

    if first:
        keep_q = pltpu.make_async_copy(wq, wq_out, sem_w.at[0])
        keep_q.start()
        keep_o = pltpu.make_async_copy(wo, wo_out, sem_w.at[1])
        keep_o.start()

    low_half = lane < 64
    blank = jnp.zeros((32, 128), BF)
    ends = []
    total = 0
    for _, ws in runs:
        total += len(ws)
        ends.append(total)

    unroll = 9 if nw % 9 == 0 else 12

    def attend_windows(step, _):
        items = [(u, g, s) for u in range(unroll) for g in range(4) for s in range(2)]
        keys, raw, outs = {}, {}, {}
        at_window = []
        for u in range(unroll):
            i = step * unroll + u
            slot = 0
            for e in ends[:-1]:
                slot = slot + jnp.where(i >= e, 1, 0)
            at_window.append((pl.ds(pl.multiple_of(i * TOK_PAD, TOK_PAD), TOK_PAD),
                              pl.multiple_of(i * 2 * D, 2 * D), slot))

        def score(u, g, s):
            r, base, _ = at_window[u]
            if s == 0:
                kh, kl = hi_lo(qkv[r, D + g * 128:D + (g + 1) * 128])
                rkh = pltpu.roll(kh, 64, 1)
                rkl = pltpu.roll(kl, 64, 1)
                keys[u, g] = (
                    jnp.concatenate([jnp.where(low_half, kh, rkl), kh[:, :64]], axis=1),
                    jnp.concatenate([jnp.where(low_half, rkh, kl), rkh[:, :64]], axis=1),
                )
            rows = []
            for part in (0, 0, D):
                at = base + part + g * 128 + 64 * s
                rows.append(jnp.concatenate([q_t[pl.ds(at, 32), :], blank], axis=1))
                rows.append(jnp.concatenate([blank, q_t[pl.ds(at + 32, 32), :]], axis=1))
            raw[u, g, s] = dot(keys[u, g][s], jnp.concatenate(rows, axis=0))

        def mix(u, g, s):
            r, base, slot = at_window[u]
            scores = raw.pop((u, g, s))
            for t in range(2):
                h = 2 * s + t
                x = scores[:, t * 128:(t + 1) * 128] + biasm[slot, g * 4 + h]
                x = jnp.exp2(x - jnp.max(x, axis=0, keepdims=True))
                inv = 1.0 / jnp.sum(x, axis=0, keepdims=True)
                hi, lo = hi_lo(x)
                at = base + g * 128 + 32 * h
                vals = jnp.concatenate([v_t[pl.ds(at, 32), :], v_t[pl.ds(at + D, 32), :]], axis=0)
                both = dot(vals[:, :TOK_PAD], jnp.concatenate([hi, lo], axis=1))
                both = both[:, :128] + both[:, 128:]
                outs.setdefault((u, g), []).append((both[:32] + both[32:]) * inv)
            if s == 1:
                hi, lo = hi_lo(jnp.concatenate(outs.pop((u, g)), axis=0).T[:TOK_PAD])
                hcat[r, g * 128:(g + 1) * 128] = hi
                hcat[r, D + g * 128:D + (g + 1) * 128] = lo

        for n in range(len(items) + AHEAD):
            if n < len(items):
                score(*items[n])
            if n >= AHEAD:
                mix(*items[n - AHEAD])
        return 0

    lax.fori_loop(0, nw // unroll, attend_windows, 0)

    if not first:
        copy_o.wait()
    for t in range(2):
        cols = slice(t * 256, (t + 1) * 256)
        proj = (dot(hcat[:, :D], wo[:D, cols]) + dot(hcat[:, D:], wo[:D, cols])
                + dot(hcat[:, :D], wo[D:, cols]))
        for i in range(nw):
            for lev in range(2):
                top = i * TOK_PAD + lev * CELL_PAD
                for g in range(2):
                    at = pl.ds(i * SLAB + (2 * t + g) * 2 + lev, CELL_PAD, stride=SUB)
                    tok[at, :] = tok[at, :] + proj[top:top + CELL_PAD, g * 128:(g + 1) * 128]
    for i in range(nw):
        move(i, dsts, False, sem_out.at[i])
    if first:
        keep_q.wait()
        keep_o.wait()
    for i in range(nw):
        there, here = whole(i, dsts)
        pltpu.make_async_copy(here, there, sem_out.at[i]).wait()


def group_call(runs, ids, tok, halos, gain, shift, w_qkv, w_out, bias, out_so_far, name):
    nw = sum(len(ws) for _, ws in runs)
    nb = len(runs)
    halo = halos is not None
    aliased = out_so_far is not None
    first = w_qkv.dtype == F32
    any_spec = pl.BlockSpec(memory_space=pl.ANY)
    hbm_spec = pl.BlockSpec(memory_space=pltpu.HBM)
    vmem_spec = pl.BlockSpec(memory_space=pltpu.VMEM)
    smem_spec = pl.BlockSpec(memory_space=pltpu.SMEM)
    args = [ids, tok]
    specs = [smem_spec, hbm_spec]
    if halo:
        args += list(halos)
        specs += [any_spec] * 3
    args += [gain, shift, w_qkv, w_out, bias]
    specs += [vmem_spec, vmem_spec, hbm_spec, hbm_spec, hbm_spec]
    aliases = {}
    if aliased:
        aliases = {len(args): 0}
        args.append(out_so_far)
        specs.append(hbm_spec)
    out_shapes = [jax.ShapeDtypeStruct(tok.shape, F32)]
    if halo:
        out_shapes += [jax.ShapeDtypeStruct(h.shape, F32) for h in halos]
    if first:
        out_shapes += [jax.ShapeDtypeStruct((2 * D, 3 * D), BF), jax.ShapeDtypeStruct((2 * D, D), BF)]
    stages = [pltpu.VMEM((D, 3 * D), F32), pltpu.VMEM((D, D), F32)] if first else []
    rows_all = nw * TOK_PAD
    return pl.pallas_call(
        functools.partial(group_kernel, runs, halo, aliased, first),
        out_shape=out_shapes,
        in_specs=specs,
        out_specs=[hbm_spec] * len(out_shapes),
        input_output_aliases=aliases,
        scratch_shapes=[
            pltpu.VMEM((nw * WIN_ROWS, WLON * SUB, 128), F32),
            pltpu.VMEM((nb, 1712, 100), F32),
            pltpu.VMEM((2 * D, 3 * D), BF),
            pltpu.VMEM((2 * D, D), BF),
            pltpu.VMEM((rows_all, 2 * D), BF),
            pltpu.VMEM((rows_all, 3 * D), F32),
            pltpu.VMEM((nw * 2 * D, 128), BF),
            pltpu.VMEM((nw * 2 * D, 128), BF),
            pltpu.VMEM((rows_all, 2 * D), BF),
            pltpu.VMEM((nb, HEADS, TOK_PAD, 128), F32),
            pltpu.SemaphoreType.DMA((nw,)),
            pltpu.SemaphoreType.DMA((TILES + 1,)),
            pltpu.SemaphoreType.DMA((nb,)),
            pltpu.SemaphoreType.DMA((nw,)),
        ] + stages,
        compiler_params=pltpu.CompilerParams(vmem_limit_bytes=(52 if halo else 56) << 20),
        cost_estimate=pl.CostEstimate(
            flops=nw * 10**9, bytes_accessed=8 << 20, transcendentals=nw * 200000),
        name=name,
    )(*args)


def rim_parts(whole_ref, s_ref, e_ref, c_ref):
    edge = HALF_LON * SUB
    return (
        (s_ref, whole_ref.at[pl.ds(0, HALF_LAT), pl.ds(edge, S_COLS * SUB)]),
        (e_ref, whole_ref.at[pl.ds(HALF_LAT, ROWS - HALF_LAT), pl.ds(0, edge)]),
        (c_ref, whole_ref.at[pl.ds(0, HALF_LAT), pl.ds(0, edge)]),
    )


def merge_kernel(s_ref, e_ref, c_ref, _, out_ref, sem):
    copies = [pltpu.make_async_copy(part, place, sem.at[n])
              for n, (part, place) in enumerate(rim_parts(out_ref, s_ref, e_ref, c_ref))]
    for c in copies:
        c.start()
    for c in copies:
        c.wait()


def pack_kernel(tok_ref, s_ref, e_ref, c_ref, sem):
    copies = [pltpu.make_async_copy(place, part, sem.at[n])
              for n, (part, place) in enumerate(rim_parts(tok_ref, s_ref, e_ref, c_ref))]
    for c in copies:
        c.start()
    for c in copies:
        c.wait()


def pack_call(tok):
    edge = HALF_LON * SUB
    return pl.pallas_call(
        pack_kernel,
        out_shape=[jax.ShapeDtypeStruct((HALF_LAT, S_COLS * SUB, 128), F32),
                   jax.ShapeDtypeStruct((ROWS - HALF_LAT, edge, 128), F32),
                   jax.ShapeDtypeStruct((HALF_LAT, edge, 128), F32)],
        in_specs=[pl.BlockSpec(memory_space=pltpu.HBM)],
        out_specs=[pl.BlockSpec(memory_space=pl.ANY)] * 3,
        scratch_shapes=[pltpu.SemaphoreType.DMA((3,))],
        compiler_params=pltpu.CompilerParams(vmem_limit_bytes=52 << 20),
        name="pack",
    )(tok)


def merge_call(s, e, c, out_so_far):
    any_spec = pl.BlockSpec(memory_space=pl.ANY)
    return pl.pallas_call(
        merge_kernel,
        out_shape=jax.ShapeDtypeStruct(out_so_far.shape, F32),
        in_specs=[any_spec] * 3 + [pl.BlockSpec(memory_space=pltpu.HBM)],
        out_specs=pl.BlockSpec(memory_space=pltpu.HBM),
        input_output_aliases={3: 0},
        scratch_shapes=[pltpu.SemaphoreType.DMA((3,))],
        compiler_params=pltpu.CompilerParams(vmem_limit_bytes=4 << 20),
        name="merge",
    )(s, e, c, out_so_far)


def shift_pairs(dlon, dlat):
    n_lon, n_lat = lax.axis_size("lon"), lax.axis_size("lat")
    pairs = []
    for lon in range(n_lon):
        for lat in range(n_lat):
            to = ((lon + dlon) % n_lon) * n_lat + (lat + dlat) % n_lat
            pairs.append((lon * n_lat + lat, to))
    return pairs


def send(value, dlon, dlat):
    return lax.ppermute(value, ("lon", "lat"), shift_pairs(dlon, dlat))


def body(tokens, ln_gain, ln_shift, w_qkv, w_out, region_ids, position_bias):
    tok = tokens.transpose(1, 2, 0, 3).reshape(ROWS, COLS, 2, 4, 128)
    tok = tok.transpose(0, 1, 3, 2, 4).reshape(ROWS, COLS * SUB, 128)
    bias = position_bias.transpose(0, 2, 1, 3).reshape(BANDS * 100 * HEADS, 100)
    s, e, c = pack_call(tok)
    s = send(s, 0, -1)
    e = send(e, -1, 0)
    c = send(c, -1, -1)
    common = (ln_gain, ln_shift, w_qkv, w_out, bias)
    inner = tuple(range(ACROSS - 1))
    out, wq, wo = group_call(((0, inner),), region_ids, tok, None, *common, None, "band0")
    common = (ln_gain, ln_shift, wq, wo, bias)
    out, s, e, c = group_call(
        ((2, tuple(range(ACROSS))), (0, (ACROSS - 1,)), (1, (ACROSS - 1,))),
        region_ids, tok, (s, e, c), *common, out, "rim")
    s = send(s, 0, 1)
    e = send(e, 1, 0)
    c = send(c, 1, 1)
    (out,) = group_call(((1, inner),), region_ids, tok, None, *common, out, "band1")
    out = merge_call(s, e, c, out)
    out = out.reshape(ROWS, COLS, 4, 2, 128).transpose(0, 1, 3, 2, 4).reshape(ROWS, COLS, 2, D)
    return out.transpose(2, 0, 1, 3)


def solution(mesh):
    in_specs = (P(None, "lat", "lon", None), P(), P(), P(), P(), P(), P("lat", None, None, None))
    out_specs = P(None, "lat", "lon", None)
    return jax.shard_map(body, mesh=mesh, in_specs=in_specs, out_specs=out_specs, check_vma=False)
```
